512 devices in a mesh: dp: 8 (over y), cent: 64 (over x, z, core).
Axes of the slice: x: 4, y: 8, z: 8, core: 2. Of those that a mesh axis runs over, the one named last changes fastest.
Arguments:
- points: bfloat16 [12288, 1024], P('dp', 'cent'), may hold values from -8 to 8
- centroids: bfloat16 [65536, 1024], P('cent'), may hold values from -0.26 to 0.26
Outputs:
- new_centroids: bfloat16 [65536, 1024], P(('cent', 'dp'))
- counts: float32 [65536], P(('cent', 'dp'))
The draws below stay inside these ranges and needn't reach their ends.
All inputs are finite; a program needn't handle non-finite values.
Results may differ from the reference program's by a relative error of at most 0.018.
Values may be sent and summed in bfloat16 or wider, within the bound.
No kernel may reach another device: no remote copies, remote signals or barrier semaphores. Data moves between devices by JAX's collectives and lax.ppermute only.
A program may use at most 64 MiB of HBM per device.

```python
import math
import jax
import jax.numpy as jnp
from jax import lax

D = 1024
KC_DEV = 1024
TOK_DEV = 1536
K = 65536
TOKENS = 12288
N_DP = 8
N_CENT = 64


def shared_centroids(key):
    entry_key = jax.random.fold_in(key, 11)
    jitter_key = jax.random.fold_in(key, 12)
    entries = jax.random.normal(entry_key, (K, D), jnp.float32) / math.sqrt(D)
    trend = 0.9 + 0.2 * jnp.arange(K, dtype=jnp.float32) / K
    jitter = jax.random.uniform(jitter_key, (K,), jnp.float32, 0.97, 1.03)
    return jnp.clip(entries * (trend * jitter)[:, None], -0.25, 0.25)


def draw_centroids(key, part):
    shared = shared_centroids(key)
    return shared.astype(jnp.bfloat16)


def draw_points(key, part):
    key = jax.random.fold_in(key, 5)
    scale_key, entry_key = jax.random.split(key, 2)
    row_scale = jnp.exp(jax.random.uniform(scale_key, (TOKENS,), jnp.float32, 0.0, math.log(10.0)))
    entries = jax.random.normal(entry_key, (TOKENS, D), jnp.float32)
    base = entries * row_scale[:, None] / math.sqrt(D)
    return jnp.clip(base, -8.0, 8.0).astype(jnp.bfloat16)


def setup_inputs(seed: int = 0) -> dict:
    seeds = jax.random.split(jax.random.key(seed), 3)
    points = draw_points(jax.random.fold_in(seeds[2], 71), 0)
    centroids = draw_centroids(jax.random.fold_in(seeds[2], 71), 0)
    return dict(points=points, centroids=centroids)


sharpness = 10.0
epsilon = 1e-12

def block_logits(points, block):
    center_norm = lax.optimization_barrier(jnp.sum(jnp.square(block.astype(jnp.float32)), axis=1))
    product = jnp.dot(points, block.T, preferred_element_type=jnp.float32)
    return sharpness * (product - 0.5 * center_norm[None, :])

def reference(points, centroids):
    blocks = centroids.reshape(N_CENT, KC_DEV, D)

    def first_pass(block):
        logits = block_logits(points, block)
        block_peak = lax.optimization_barrier(jnp.max(logits, axis=1))
        block_total = lax.optimization_barrier(jnp.sum(jnp.exp(logits - block_peak[:, None]), axis=1))
        return (block_peak, block_total)
    peaks, totals = lax.map(first_pass, blocks)
    row_peak = lax.optimization_barrier(jnp.max(peaks, axis=0))
    row_total = lax.optimization_barrier(jnp.sum(totals * jnp.exp(peaks - row_peak[None, :]), axis=0))
    data = points.reshape(N_DP, TOK_DEV, D).astype(jnp.float32)

    def second_pass(block):
        logits = block_logits(points, block)
        responsibility = (jnp.exp(logits - row_peak[:, None]) / row_total[:, None]).astype(jnp.bfloat16)
        grouped = responsibility.reshape(N_DP, TOK_DEV, KC_DEV).astype(jnp.float32)
        part_sums = jnp.einsum('npk,npd->nkd', grouped, data, precision=lax.Precision.HIGHEST).astype(jnp.bfloat16)
        part_sums = lax.optimization_barrier(part_sums)
        part_counts = lax.optimization_barrier(jnp.sum(grouped, axis=1)).astype(jnp.bfloat16)
        part_counts = lax.optimization_barrier(part_counts)
        sums = lax.optimization_barrier(jnp.sum(part_sums.astype(jnp.float32), axis=0))
        raw_counts = lax.optimization_barrier(jnp.sum(part_counts.astype(jnp.float32), axis=0))
        row_scale = lax.rsqrt(lax.optimization_barrier(jnp.mean(sums * sums, axis=1, keepdims=True)) + epsilon)
        fresh = (sums * row_scale).astype(jnp.bfloat16)
        return (fresh, raw_counts * (KC_DEV * N_CENT / TOKENS))
    fresh, counts = lax.map(second_pass, blocks)
    return (fresh.reshape(K, D), counts.reshape(K))
```

```python
import functools

import jax
import jax.numpy as jnp
from jax import lax
from jax.experimental import pallas as pl
from jax.experimental.pallas import tpu as pltpu
from jax.sharding import PartitionSpec as P

sharpness = 10.0
epsilon = 1e-12
lanes = 128
tile = 256
tall = 512
vmem = pl.BlockSpec(memory_space=pltpu.VMEM)
smem = pl.BlockSpec(memory_space=pltpu.SMEM)
hbm = pl.BlockSpec(memory_space=pltpu.HBM)


def limit(mib):
    return pltpu.CompilerParams(vmem_limit_bytes=mib << 20)


def logits_kernel(cent_ref, source_ref, points_ref, raised_ref, peak_ref, lse_ref, norm_ref, sems):
    n_cent, n_tok = raised_ref.shape
    row_blocks = [pl.ds(r, tall) for r in range(0, n_cent, tall)]
    token_blocks = [pl.ds(t, tile) for t in range(0, n_tok, tile)]
    copies = [
        pltpu.make_async_copy(source_ref.at[:, cols], points_ref.at[:, cols], sems.at[i])
        for i, cols in enumerate(token_blocks)
    ]
    for copy in copies:
        copy.start()
    for rows in row_blocks:
        entries = cent_ref[rows, :].astype(jnp.float32)
        half_norm = 0.5 * jnp.sum(entries * entries, axis=1, keepdims=True)
        norm_ref[rows, :] = jnp.broadcast_to(half_norm, (tall, lanes))
    peaks = []
    for step in range(len(token_blocks) + 1):
        if step < len(token_blocks):
            copies[step].wait()
        tops, totals = [], []
        for rows in row_blocks:
            if step < len(token_blocks):
                cols = token_blocks[step]
                product = jnp.dot(
                    cent_ref[rows, :], points_ref[:, cols], preferred_element_type=jnp.float32
                )
                logits = sharpness * (product - norm_ref[rows, :1])
                raised_ref[rows, cols] = logits
                tops.append(jnp.max(logits, axis=0, keepdims=True))
            if step > 0:
                cols = token_blocks[step - 1]
                raised = jnp.exp(raised_ref[rows, cols] - peaks[step - 1])
                raised_ref[rows, cols] = raised
                totals.append(jnp.sum(raised, axis=0, keepdims=True))
        if step < len(token_blocks):
            peaks.append(functools.reduce(jnp.maximum, tops))
            peak_ref[:, token_blocks[step]] = peaks[step]
        if step > 0:
            lse_ref[:, token_blocks[step - 1]] = peaks[step - 1] + jnp.log(sum(totals))


def local_softmax(centroids, points):
    n_cent, n_tok = centroids.shape[0], points.shape[1]
    row = jax.ShapeDtypeStruct((1, n_tok), jnp.float32)
    raised = jax.ShapeDtypeStruct((n_cent, n_tok), jnp.float32)
    return pl.pallas_call(
        logits_kernel,
        out_shape=(jax.ShapeDtypeStruct(points.shape, points.dtype), raised, row, row),
        in_specs=[vmem, hbm],
        out_specs=[vmem] * 4,
        scratch_shapes=[
            pltpu.VMEM((n_cent, lanes), jnp.float32), pltpu.SemaphoreType.DMA((n_tok // tile,)),
        ],
        compiler_params=limit(12),
        cost_estimate=pl.CostEstimate(
            flops=2 * centroids.size * n_tok, bytes_accessed=8 * n_cent * n_tok,
            transcendentals=n_cent * n_tok,
        ),
        name="local_softmax",
    )(centroids, points)


def sums_kernel(order, n_blocks, place_ref, lse_ref, *refs):
    halves, outs, resp_ref = (refs[0:3], refs[3:6]), refs[6:-1], refs[-1]
    share, width = outs[-1].shape
    depth = width - lanes
    far = len(outs) - len(order)
    cut = outs[0].shape[1]
    n_tok = refs[0].shape[1]

    def put(i, start, value):
        value = value.astype(jnp.bfloat16)
        if i > 0 or not far:
            outs[i + far][:, pl.ds(start, value.shape[1])] = value
        elif start < cut:
            outs[0][:, pl.ds(start, value.shape[1])] = value
        else:
            outs[1][:, pl.ds(start - cut, value.shape[1])] = value

    parts = lse_ref[...]
    top = jnp.max(parts, axis=0, keepdims=True)
    norm = top + jnp.log(jnp.sum(jnp.exp(parts - top), axis=0, keepdims=True))
    scales = [
        jnp.exp(half[1][...] - norm[:, h * n_tok:(h + 1) * n_tok]) for h, half in enumerate(halves)
    ]
    for i, d in enumerate(order):
        start = lax.rem(place_ref[0] + d + n_blocks, n_blocks) * share
        rows = pl.ds(pl.multiple_of(start, share), share)
        count = jnp.zeros((share, 1), jnp.float32)
        for h, half in enumerate(halves):
            resp = (half[0][rows, :] * scales[h]).astype(jnp.bfloat16)
            resp_ref[pl.ds(i * share, share), pl.ds(h * n_tok, n_tok)] = resp
            count += jnp.sum(resp.astype(jnp.float32), axis=1, keepdims=True)
        put(i, depth, jnp.broadcast_to(count, (share, lanes)))
    for i in range(0, len(order), tall // share):
        rows = min(tall, (len(order) - i) * share)
        for c in range(0, depth, tile):
            total = sum(
                lax.dot_general(
                    resp_ref[pl.ds(i * share, rows), pl.ds(h * n_tok, n_tok)],
                    half[2][pl.ds(c, tile), :],
                    (((1,), (1,)), ((), ())),
                    preferred_element_type=jnp.float32,
                )
                for h, half in enumerate(halves)
            )
            for k in range(rows // share):
                put(i + k, c, total[k * share:(k + 1) * share])


def weighted_sums(order, n_blocks, far, place, lse, halves):
    n_cent, n_tok = halves[0][0].shape
    depth = halves[0][2].shape[0]
    n = len(order)
    share, cut = n_cent // n_blocks, depth // 2
    widths = ((cut, depth + lanes - cut) if far else (depth + lanes,)) + (depth + lanes,) * (n - 1)
    return pl.pallas_call(
        functools.partial(sums_kernel, order, n_blocks),
        out_shape=tuple(jax.ShapeDtypeStruct((share, w), jnp.bfloat16) for w in widths),
        in_specs=[smem] + [vmem] * 7,
        out_specs=(vmem,) * len(widths),
        scratch_shapes=[pltpu.VMEM((n * share, 2 * n_tok), jnp.bfloat16)],
        compiler_params=limit(20),
        cost_estimate=pl.CostEstimate(
            flops=4 * n * share * n_tok * depth, bytes_accessed=16 * n * share * n_tok, transcendentals=0
        ),
        name="weighted_sums",
    )(place, lse, *halves[0], *halves[1])


def finish_kernel(factor, own_ref, down_ref, up_ref, fresh_ref, counts_ref):
    total = sum(ref[...].astype(jnp.float32) for ref in (own_ref, down_ref, up_ref))
    depth = fresh_ref.shape[1]
    sums = total[:, :depth]
    mean = jnp.sum(sums * sums, axis=1, keepdims=True) / depth
    fresh_ref[...] = (sums * lax.rsqrt(mean + epsilon)).astype(fresh_ref.dtype)
    counts_ref[...] = jnp.transpose(total[:, depth:] * factor)[:1]


def finish(own, down, up, factor):
    share, width = own.shape
    fresh, counts = pl.pallas_call(
        functools.partial(finish_kernel, factor),
        out_shape=(
            jax.ShapeDtypeStruct((share, width - lanes), jnp.bfloat16),
            jax.ShapeDtypeStruct((1, share), jnp.float32),
        ),
        in_specs=[vmem] * 3,
        out_specs=[vmem] * 2,
        compiler_params=limit(4),
        name="finish",
    )(own, down, up)
    return fresh, counts.reshape(share)


def core_swap(value):
    return lax.ppermute(value, "core", [(0, 1), (1, 0)])


def spread(value, axis):
    n = lax.psum(1, axis)
    return lax.all_to_all(jnp.broadcast_to(value[None], (n,) + value.shape), axis, 0, 0)


def gather_half(points):
    n_tok, cols = points.shape
    n_z, n_core = lax.axis_size("z"), lax.axis_size("core")
    part, rows = n_tok // n_core, points.T
    halves = jnp.stack([rows[:, c * part:(c + 1) * part] for c in range(n_core)])
    blocks = jnp.broadcast_to(halves[None], (n_z,) + halves.shape).reshape((n_z * n_core,) + halves.shape[1:])
    slab = lax.all_to_all(blocks, ("z", "core"), 0, 0).reshape(-1, n_tok // n_core)
    return spread(slab, "x").reshape(-1, n_tok // n_core)


def dp_shift(value, d):
    n = lax.axis_size("dp")
    return lax.ppermute(value, "dp", [((i + d) % n, i) for i in range(n)])


def ring_order(n):
    near = [s * d for d in range(n // 2 - 1, 0, -1) for s in (-1, 1)]
    return [n // 2] + near + [0]


def add(block, total, start):
    stop = start + total.shape[1]
    part = block[:, start:stop].astype(jnp.float32) + total.astype(jnp.float32)
    pieces = [block[:, :start], part.astype(block.dtype), block[:, stop:]]
    return jnp.concatenate([p for p in pieces if p.shape[1]], axis=1)


def ring_sum(far, near, make_rest):
    down, up = dp_shift(far[0], 1), dp_shift(far[1], -1)
    starts = 0, far[0].shape[1]
    rest = make_rest(up)
    while len(near) > 1:
        down = dp_shift(add(near[0], down, starts[0]), 1)
        up = dp_shift(add(near[1], up, starts[1]), -1)
        near, rest = (near[2:] or rest), (rest if near[2:] else ())
        starts = 0, 0
    return near[0], down, up


def per_device(points, centroids):
    n_dp = lax.axis_size("dp")
    n_cent = lax.axis_size("x") * lax.axis_size("z") * lax.axis_size("core")
    place = lax.axis_index("dp").astype(jnp.int32).reshape(1)
    points, place = lax.optimization_barrier((points, place))
    mine = gather_half(points)
    other = core_swap(mine)
    points_0, raised_0, peak_0, lse_0 = local_softmax(centroids, mine)
    points_1, raised_1, peak_1, lse_1 = local_softmax(centroids, other)
    here = jnp.concatenate([lse_0, lse_1], axis=1)
    there = core_swap(jnp.concatenate([lse_1, lse_0], axis=1))
    lse = spread(jnp.logaddexp(here, there)[0], ("x", "z"))
    halves = ((raised_0, peak_0, points_0), (raised_1, peak_1, points_1))
    order = ring_order(n_dp)
    first = weighted_sums(order[:3], n_dp, True, place, lse, halves)

    def make_rest(after):
        late, _ = lax.optimization_barrier((lse, after))
        return weighted_sums(order[3:], n_dp, False, place, late, halves)

    own, down, up = ring_sum(first[:2], first[2:], make_rest)
    factor = centroids.shape[0] * n_cent / (points.shape[0] * n_dp)
    return finish(own, down, up, factor)


def solution(mesh):
    n_dp = mesh.shape["dp"]
    split = (4, mesh.shape["cent"] // 8, 2)
    fine = jax.sharding.Mesh(mesh.devices.reshape((n_dp,) + split), ("dp", "x", "z", "core"))
    cent = ("x", "z", "core")
    in_specs = (P("dp", cent), P(cent, None))
    out_specs = (P(cent + ("dp",), None), P(cent + ("dp",)))
    return jax.shard_map(
        per_device, mesh=fine, in_specs=in_specs, out_specs=out_specs, check_vma=False
    )
```

```python
import functools

import jax
import jax.numpy as jnp
from jax import lax
from jax.experimental import pallas as pl
from jax.experimental.pallas import tpu as pltpu
from jax.sharding import PartitionSpec as P

sharpness = 10.0
epsilon = 1e-12
lanes = 128
tile = 256
tall = 512
count_rows = 16
vmem = pl.BlockSpec(memory_space=pltpu.VMEM)
smem = pl.BlockSpec(memory_space=pltpu.SMEM)


def limit(mib):
    return pltpu.CompilerParams(vmem_limit_bytes=mib << 20)


def norms_kernel(cent_ref, points_ref, *refs):
    norm_ref = refs[-1]
    for r in range(0, cent_ref.shape[0], tall):
        rows = pl.ds(r, tall)
        entries = cent_ref[rows, :].astype(jnp.float32)
        half_norm = 0.5 * jnp.sum(entries * entries, axis=1, keepdims=True)
        norm_ref[rows, :] = jnp.broadcast_to(half_norm, (tall, lanes))
    logits_kernel(cent_ref, points_ref, norm_ref, *refs[:-1])


def logits_kernel(cent_ref, points_ref, norm_ref, raised_ref, peak_ref, lse_ref):
    n_cent, n_tok = raised_ref.shape
    row_blocks = [pl.ds(r, tall) for r in range(0, n_cent, tall)]
    token_blocks = [pl.ds(t, tile) for t in range(0, n_tok, tile)]
    peaks = []
    for step in range(len(token_blocks) + 1):
        tops, totals = [], []
        for rows in row_blocks:
            if step < len(token_blocks):
                cols = token_blocks[step]
                product = jnp.dot(
                    cent_ref[rows, :], points_ref[:, cols], preferred_element_type=jnp.float32
                )
                logits = sharpness * (product - norm_ref[rows, :1])
                raised_ref[rows, cols] = logits
                tops.append(jnp.max(logits, axis=0, keepdims=True))
            if step > 0:
                cols = token_blocks[step - 1]
                raised = jnp.exp(raised_ref[rows, cols] - peaks[step - 1])
                raised_ref[rows, cols] = raised
                totals.append(jnp.sum(raised, axis=0, keepdims=True))
        if step < len(token_blocks):
            peaks.append(functools.reduce(jnp.maximum, tops))
            peak_ref[:, token_blocks[step]] = peaks[step]
        if step > 0:
            lse_ref[:, token_blocks[step - 1]] = peaks[step - 1] + jnp.log(sum(totals))


def local_softmax(centroids, points, norms=None):
    n_cent, n_tok = centroids.shape[0], points.shape[1]
    row = jax.ShapeDtypeStruct((1, n_tok), jnp.float32)
    outs = (jax.ShapeDtypeStruct((n_cent, n_tok), jnp.float32), row, row)
    if norms is None:
        outs += (jax.ShapeDtypeStruct((n_cent, lanes), jnp.float32),)
    operands = (centroids, points) + (() if norms is None else (norms,))
    results = pl.pallas_call(
        norms_kernel if norms is None else logits_kernel,
        out_shape=outs,
        in_specs=[vmem] * len(operands),
        out_specs=[vmem] * len(outs),
        compiler_params=limit(12),
        cost_estimate=pl.CostEstimate(
            flops=2 * centroids.size * n_tok, bytes_accessed=8 * n_cent * n_tok,
            transcendentals=n_cent * n_tok,
        ),
        name="local_softmax",
    )(*operands)
    return results if norms is None else (*results, norms)


def sums_kernel(order, n_blocks, place_ref, lse_ref, *refs):
    halves, outs, resp_ref = (refs[0:3], refs[3:6]), refs[6:-1], refs[-1]
    depth = halves[0][2].shape[0]
    share = refs[0].shape[0] // n_blocks
    n_tok = refs[0].shape[1]
    far = len(outs) - len(order)
    cut = outs[0].shape[0]

    def put(i, start, value):
        value = value.astype(jnp.bfloat16)
        if i > 0 or not far:
            outs[i + far][pl.ds(start, value.shape[0]), :] = value
        elif start < cut:
            outs[0][pl.ds(start, value.shape[0]), :] = value
        else:
            outs[1][pl.ds(start - cut, value.shape[0]), :] = value

    parts = lse_ref[...]
    top = jnp.max(parts, axis=0, keepdims=True)
    norm = top + jnp.log(jnp.sum(jnp.exp(parts - top), axis=0, keepdims=True))
    scales = [
        jnp.exp(half[1][...] - norm[:, h * n_tok:(h + 1) * n_tok]) for h, half in enumerate(halves)
    ]
    for i, d in enumerate(order):
        start = lax.rem(place_ref[0] + d + n_blocks, n_blocks) * share
        rows = pl.ds(pl.multiple_of(start, share), share)
        count = jnp.zeros((share, 1), jnp.float32)
        for h, half in enumerate(halves):
            resp = (half[0][rows, :] * scales[h]).astype(jnp.bfloat16)
            resp_ref[pl.ds(i * share, share), pl.ds(h * n_tok, n_tok)] = resp
            count += jnp.sum(resp.astype(jnp.float32), axis=1, keepdims=True)
        put(i, depth // lanes * share, jnp.transpose(jnp.broadcast_to(count, (share, lanes)))[:count_rows])
    for i in range(0, len(order), tall // share):
        rows = min(tall, (len(order) - i) * share)
        for c in range(0, depth, tile):
            total = sum(
                lax.dot_general(
                    resp_ref[pl.ds(i * share, rows), pl.ds(h * n_tok, n_tok)],
                    half[2][pl.ds(c, tile), :],
                    (((1,), (1,)), ((), ())),
                    preferred_element_type=jnp.float32,
                )
                for h, half in enumerate(halves)
            )
            for k in range(rows // share):
                for p in range(0, tile, lanes):
                    put(i + k, (c + p) // lanes * share, total[k * share:(k + 1) * share, p:p + lanes])


def weighted_sums(order, n_blocks, far, place, lse, halves):
    n_cent, n_tok = halves[0][0].shape
    depth = halves[0][2].shape[0]
    n = len(order)
    share = n_cent // n_blocks
    height, cut = depth // lanes * share + count_rows, depth // lanes // 2 * share
    heights = ((cut, height - cut) if far else (height,)) + (height,) * (n - 1)
    return pl.pallas_call(
        functools.partial(sums_kernel, order, n_blocks),
        out_shape=tuple(jax.ShapeDtypeStruct((h, lanes), jnp.bfloat16) for h in heights),
        in_specs=[smem] + [vmem] * 7,
        out_specs=(vmem,) * len(heights),
        scratch_shapes=[pltpu.VMEM((n * share, 2 * n_tok), jnp.bfloat16)],
        compiler_params=limit(20),
        cost_estimate=pl.CostEstimate(
            flops=4 * n * share * n_tok * depth, bytes_accessed=16 * n * share * n_tok, transcendentals=0
        ),
        name="weighted_sums",
    )(place, lse, *halves[0], *halves[1])


def finish_kernel(factor, own_ref, down_ref, up_ref, fresh_ref, counts_ref):
    share, depth = fresh_ref.shape

    def total(start, size):
        rows = pl.ds(start, size)
        return sum(ref[rows, :].astype(jnp.float32) for ref in (own_ref, down_ref, up_ref))

    pieces = [total(c // lanes * share, share) for c in range(0, depth, lanes)]
    mean = jnp.sum(sum(piece * piece for piece in pieces), axis=1, keepdims=True) / depth
    scale = lax.rsqrt(mean + epsilon)
    for i, piece in enumerate(pieces):
        fresh_ref[:, pl.ds(i * lanes, lanes)] = (piece * scale).astype(fresh_ref.dtype)
    counts_ref[...] = total(depth // lanes * share, count_rows)[:1] * factor


def finish(own, down, up, share, depth, factor):
    fresh, counts = pl.pallas_call(
        functools.partial(finish_kernel, factor),
        out_shape=(
            jax.ShapeDtypeStruct((share, depth), jnp.bfloat16),
            jax.ShapeDtypeStruct((1, share), jnp.float32),
        ),
        in_specs=[vmem] * 3,
        out_specs=[vmem] * 2,
        compiler_params=limit(4),
        name="finish",
    )(own, down, up)
    return fresh, counts.reshape(share)


def core_swap(value):
    return lax.ppermute(value, "core", [(0, 1), (1, 0)])


def spread(value, axis):
    n = lax.psum(1, axis)
    return lax.all_to_all(jnp.broadcast_to(value[None], (n,) + value.shape), axis, 0, 0)


def gather_half(points):
    n_tok, cols = points.shape
    n_z, n_core = lax.axis_size("z"), lax.axis_size("core")
    part, rows = n_tok // n_core, points.T
    halves = jnp.stack([rows[:, c * part:(c + 1) * part] for c in range(n_core)])
    blocks = jnp.broadcast_to(halves[None], (n_z,) + halves.shape).reshape((n_z * n_core,) + halves.shape[1:])
    slab = lax.all_to_all(blocks, ("z", "core"), 0, 0).reshape(-1, n_tok // n_core)
    return spread(slab, "x").reshape(-1, n_tok // n_core)


def dp_shift(value, d):
    n = lax.axis_size("dp")
    return lax.ppermute(value, "dp", [((i + d) % n, i) for i in range(n)])


def ring_order(n):
    near = [s * d for d in range(n // 2 - 1, 0, -1) for s in (-1, 1)]
    return [n // 2] + near + [0]


def add(block, total, start):
    stop = start + total.shape[0]
    part = block[start:stop].astype(jnp.float32) + total.astype(jnp.float32)
    pieces = [block[:start], part.astype(block.dtype), block[stop:]]
    return jnp.concatenate([p for p in pieces if p.shape[0]], axis=0)


def ring_sum(far, near, make_rest):
    down, up = dp_shift(far[0], 1), dp_shift(far[1], -1)
    starts = 0, far[0].shape[0]
    rest = make_rest(up)
    while len(near) > 1:
        down = dp_shift(add(near[0], down, starts[0]), 1)
        up = dp_shift(add(near[1], up, starts[1]), -1)
        near, rest = (near[2:] or rest), (rest if near[2:] else ())
        starts = 0, 0
    return near[0], down, up


def per_device(points, centroids):
    n_dp = lax.axis_size("dp")
    n_cent = lax.axis_size("x") * lax.axis_size("z") * lax.axis_size("core")
    place = lax.axis_index("dp").astype(jnp.int32).reshape(1)
    points, place = lax.optimization_barrier((points, place))
    mine = gather_half(points)
    other = core_swap(mine)
    raised_0, peak_0, lse_0, norms = local_softmax(centroids, mine)
    raised_1, peak_1, lse_1, _ = local_softmax(centroids, other, norms)
    here = jnp.concatenate([lse_0, lse_1], axis=1)
    there = core_swap(jnp.concatenate([lse_1, lse_0], axis=1))
    lse = spread(jnp.logaddexp(here, there)[0], ("x", "z"))
    halves = ((raised_0, peak_0, mine), (raised_1, peak_1, other))
    order = ring_order(n_dp)
    first = weighted_sums(order[:3], n_dp, True, place, lse, halves)

    def make_rest(after):
        late, _ = lax.optimization_barrier((lse, after))
        return weighted_sums(order[3:], n_dp, False, place, late, halves)

    own, down, up = ring_sum(first[:2], first[2:], make_rest)
    factor = centroids.shape[0] * n_cent / (points.shape[0] * n_dp)
    return finish(own, down, up, centroids.shape[0] // n_dp, centroids.shape[1], factor)


def solution(mesh):
    n_dp = mesh.shape["dp"]
    split = (4, mesh.shape["cent"] // 8, 2)
    fine = jax.sharding.Mesh(mesh.devices.reshape((n_dp,) + split), ("dp", "x", "z", "core"))
    cent = ("x", "z", "core")
    in_specs = (P("dp", cent), P(cent, None))
    out_specs = (P(cent + ("dp",), None), P(cent + ("dp",)))
    return jax.shard_map(
        per_device, mesh=fine, in_specs=in_specs, out_specs=out_specs, check_vma=False
    )
```

```python
import functools

import jax
import jax.numpy as jnp
from jax import lax
from jax.experimental import pallas as pl
from jax.experimental.pallas import tpu as pltpu
from jax.sharding import PartitionSpec as P

sharpness = 10.0
epsilon = 1e-12
lanes = 128
tile = 256
tall = 512
count_rows = 16
vmem = pl.BlockSpec(memory_space=pltpu.VMEM)
smem = pl.BlockSpec(memory_space=pltpu.SMEM)


def limit(mib):
    return pltpu.CompilerParams(vmem_limit_bytes=mib << 20)


def norms_kernel(cent_ref, points_ref, *refs):
    norm_ref = refs[-1]
    for r in range(0, cent_ref.shape[0], tall):
        rows = pl.ds(r, tall)
        entries = cent_ref[rows, :].astype(jnp.float32)
        half_norm = 0.5 * jnp.sum(entries * entries, axis=1, keepdims=True)
        norm_ref[rows, :] = jnp.broadcast_to(half_norm, (tall, lanes))
    logits_kernel(cent_ref, points_ref, norm_ref, *refs[:-1])


def logits_kernel(cent_ref, points_ref, norm_ref, raised_ref, peak_ref, lse_ref):
    n_cent, n_tok = raised_ref.shape
    row_blocks = [pl.ds(r, tall) for r in range(0, n_cent, tall)]
    token_blocks = [pl.ds(t, tile) for t in range(0, n_tok, tile)]
    peaks = []
    for step in range(len(token_blocks) + 1):
        tops, totals = [], []
        for rows in row_blocks:
            if step < len(token_blocks):
                cols = token_blocks[step]
                product = jnp.dot(
                    cent_ref[rows, :], points_ref[:, cols], preferred_element_type=jnp.float32
                )
                logits = sharpness * (product - norm_ref[rows, :1])
                raised_ref[rows, cols] = logits
                tops.append(jnp.max(logits, axis=0, keepdims=True))
            if step > 0:
                cols = token_blocks[step - 1]
                raised = jnp.exp(raised_ref[rows, cols] - peaks[step - 1])
                raised_ref[rows, cols] = raised
                totals.append(jnp.sum(raised, axis=0, keepdims=True))
        if step < len(token_blocks):
            peaks.append(functools.reduce(jnp.maximum, tops))
            peak_ref[:, token_blocks[step]] = peaks[step]
        if step > 0:
            lse_ref[:, token_blocks[step - 1]] = peaks[step - 1] + jnp.log(sum(totals))


def local_softmax(centroids, points, norms=None):
    n_cent, n_tok = centroids.shape[0], points.shape[1]
    row = jax.ShapeDtypeStruct((1, n_tok), jnp.float32)
    outs = (jax.ShapeDtypeStruct((n_cent, n_tok), jnp.float32), row, row)
    if norms is None:
        outs += (jax.ShapeDtypeStruct((n_cent, lanes), jnp.float32),)
    operands = (centroids, points) + (() if norms is None else (norms,))
    results = pl.pallas_call(
        norms_kernel if norms is None else logits_kernel,
        out_shape=outs,
        in_specs=[vmem] * len(operands),
        out_specs=[vmem] * len(outs),
        compiler_params=limit(12),
        cost_estimate=pl.CostEstimate(
            flops=2 * centroids.size * n_tok, bytes_accessed=8 * n_cent * n_tok,
            transcendentals=n_cent * n_tok,
        ),
        name="local_softmax",
    )(*operands)
    return results if norms is None else (*results, norms)


def sums_kernel(order, n_blocks, place_ref, lse_ref, *refs):
    halves, outs, resp_ref = (refs[0:3], refs[3:6]), refs[6:-1], refs[-1]
    depth = halves[0][2].shape[0]
    share = refs[0].shape[0] // n_blocks
    n_tok = refs[0].shape[1]
    far = len(outs) - len(order)
    cut = outs[0].shape[0]

    def put(i, start, value):
        value = value.astype(jnp.bfloat16)
        if i > 0 or not far:
            outs[i + far][pl.ds(start, value.shape[0]), :] = value
        elif start < cut:
            outs[0][pl.ds(start, value.shape[0]), :] = value
        else:
            outs[1][pl.ds(start - cut, value.shape[0]), :] = value

    parts = lse_ref[...]
    top = jnp.max(parts, axis=0, keepdims=True)
    norm = top + jnp.log(jnp.sum(jnp.exp(parts - top), axis=0, keepdims=True))
    scales = [
        jnp.exp(half[1][...] - norm[:, h * n_tok:(h + 1) * n_tok]) for h, half in enumerate(halves)
    ]
    for i, d in enumerate(order):
        start = lax.rem(place_ref[0] + d + n_blocks, n_blocks) * share
        rows = pl.ds(pl.multiple_of(start, share), share)
        count = jnp.zeros((share, 1), jnp.float32)
        for h, half in enumerate(halves):
            resp = (half[0][rows, :] * scales[h]).astype(jnp.bfloat16)
            resp_ref[pl.ds(i * share, share), pl.ds(h * n_tok, n_tok)] = resp
            count += jnp.sum(resp.astype(jnp.float32), axis=1, keepdims=True)
        put(i, depth // lanes * share, jnp.transpose(jnp.broadcast_to(count, (share, lanes)))[:count_rows])
    for i in range(0, len(order), tall // share):
        rows = min(tall, (len(order) - i) * share)
        for c in range(0, depth, tile):
            total = sum(
                lax.dot_general(
                    resp_ref[pl.ds(i * share, rows), pl.ds(h * n_tok, n_tok)],
                    half[2][pl.ds(c, tile), :],
                    (((1,), (1,)), ((), ())),
                    preferred_element_type=jnp.float32,
                )
                for h, half in enumerate(halves)
            )
            for k in range(rows // share):
                for p in range(0, tile, lanes):
                    put(i + k, (c + p) // lanes * share, total[k * share:(k + 1) * share, p:p + lanes])


def weighted_sums(order, n_blocks, far, place, lse, halves):
    n_cent, n_tok = halves[0][0].shape
    depth = halves[0][2].shape[0]
    n = len(order)
    share = n_cent // n_blocks
    height, cut = depth // lanes * share + count_rows, depth // lanes // 2 * share
    heights = ((cut, height - cut) if far else (height,)) + (height,) * (n - 1)
    return pl.pallas_call(
        functools.partial(sums_kernel, order, n_blocks),
        out_shape=tuple(jax.ShapeDtypeStruct((h, lanes), jnp.bfloat16) for h in heights),
        in_specs=[smem] + [vmem] * 7,
        out_specs=(vmem,) * len(heights),
        scratch_shapes=[pltpu.VMEM((n * share, 2 * n_tok), jnp.bfloat16)],
        compiler_params=limit(20),
        cost_estimate=pl.CostEstimate(
            flops=4 * n * share * n_tok * depth, bytes_accessed=16 * n * share * n_tok, transcendentals=0
        ),
        name="weighted_sums",
    )(place, lse, *halves[0], *halves[1])


def finish_kernel(factor, own_ref, down_ref, up_ref, fresh_ref, counts_ref):
    share, depth = fresh_ref.shape

    def total(start, size):
        rows = pl.ds(start, size)
        return sum(ref[rows, :].astype(jnp.float32) for ref in (own_ref, down_ref, up_ref))

    pieces = [total(c // lanes * share, share) for c in range(0, depth, lanes)]
    mean = jnp.sum(sum(piece * piece for piece in pieces), axis=1, keepdims=True) / depth
    scale = lax.rsqrt(mean + epsilon)
    for i, piece in enumerate(pieces):
        fresh_ref[:, pl.ds(i * lanes, lanes)] = (piece * scale).astype(fresh_ref.dtype)
    counts_ref[...] = total(depth // lanes * share, count_rows)[:1] * factor


def finish(own, down, up, share, depth, factor):
    fresh, counts = pl.pallas_call(
        functools.partial(finish_kernel, factor),
        out_shape=(
            jax.ShapeDtypeStruct((share, depth), jnp.bfloat16),
            jax.ShapeDtypeStruct((1, share), jnp.float32),
        ),
        in_specs=[vmem] * 3,
        out_specs=[vmem] * 2,
        compiler_params=limit(4),
        name="finish",
    )(own, down, up)
    return fresh, counts.reshape(share)


def core_swap(value):
    return lax.ppermute(value, "core", [(0, 1), (1, 0)])


def spread(value, axis):
    n = lax.psum(1, axis)
    return lax.all_to_all(jnp.broadcast_to(value[None], (n,) + value.shape), axis, 0, 0)


def gather_half(points):
    n_tok, cols = points.shape
    n_z, n_core = lax.axis_size("z"), lax.axis_size("core")
    part, rows = n_tok // n_core, points.T
    halves = jnp.stack([rows[:, c * part:(c + 1) * part] for c in range(n_core)])
    blocks = jnp.broadcast_to(halves[None], (n_z,) + halves.shape).reshape((n_z * n_core,) + halves.shape[1:])
    slab = lax.all_to_all(blocks, ("z", "core"), 0, 0).reshape(-1, n_tok // n_core)
    return spread(slab, "x").reshape(-1, n_tok // n_core)


def dp_shift(value, d):
    n = lax.axis_size("dp")
    return lax.ppermute(value, "dp", [((i + d) % n, i) for i in range(n)])


def ring_order(n):
    near = [s * d for d in range(n // 2 - 1, 0, -1) for s in (-1, 1)]
    return [n // 2] + near + [0]


def add(block, total, start):
    stop = start + total.shape[0]
    part = block[start:stop].astype(jnp.float32) + total.astype(jnp.float32)
    pieces = [block[:start], part.astype(block.dtype), block[stop:]]
    return jnp.concatenate([p for p in pieces if p.shape[0]], axis=0)


def ring_sum(far, near, make_rest):
    down, up = dp_shift(far[0], 1), dp_shift(far[1], -1)
    starts = 0, far[0].shape[0]
    while len(near) > 1:
        rest = make_rest(up) if len(near) == 2 else near[2:]
        down = dp_shift(add(near[0], down, starts[0]), 1)
        up = dp_shift(add(near[1], up, starts[1]), -1)
        near = rest
        starts = 0, 0
    return near[0], down, up


def per_device(points, centroids):
    n_dp = lax.axis_size("dp")
    n_cent = lax.axis_size("x") * lax.axis_size("z") * lax.axis_size("core")
    place = lax.axis_index("dp").astype(jnp.int32).reshape(1)
    points, place = lax.optimization_barrier((points, place))
    mine = gather_half(points)
    other = core_swap(mine)
    raised_0, peak_0, lse_0, norms = local_softmax(centroids, mine)
    raised_1, peak_1, lse_1, _ = local_softmax(centroids, other, norms)
    here = jnp.concatenate([lse_0, lse_1], axis=1)
    there = core_swap(jnp.concatenate([lse_1, lse_0], axis=1))
    lse = spread(jnp.logaddexp(here, there)[0], ("x", "z"))
    halves = ((raised_0, peak_0, mine), (raised_1, peak_1, other))
    order = ring_order(n_dp)
    first = weighted_sums(order[:3], n_dp, True, place, lse, halves)
    rounds = [order[i:i + 2] for i in range(3, n_dp - 3, 2)] + [order[-3:]]

    def make_rest(after):
        late, _ = lax.optimization_barrier((lse, after))
        return weighted_sums(rounds.pop(0), n_dp, False, place, late, halves)

    own, down, up = ring_sum(first[:2], first[2:], make_rest)
    factor = centroids.shape[0] * n_cent / (points.shape[0] * n_dp)
    return finish(own, down, up, centroids.shape[0] // n_dp, centroids.shape[1], factor)


def solution(mesh):
    n_dp = mesh.shape["dp"]
    split = (4, mesh.shape["cent"] // 8, 2)
    fine = jax.sharding.Mesh(mesh.devices.reshape((n_dp,) + split), ("dp", "x", "z", "core"))
    cent = ("x", "z", "core")
    in_specs = (P("dp", cent), P(cent, None))
    out_specs = (P(cent + ("dp",), None), P(cent + ("dp",)))
    return jax.shard_map(
        per_device, mesh=fine, in_specs=in_specs, out_specs=out_specs, check_vma=False
    )
```

```python
import functools

import jax
import jax.numpy as jnp
from jax import lax
from jax.experimental import pallas as pl
from jax.experimental.pallas import tpu as pltpu
from jax.sharding import PartitionSpec as P

sharpness = 10.0
epsilon = 1e-12
lanes = 128
tile = 256
tall = 512
count_rows = 16
vmem = pl.BlockSpec(memory_space=pltpu.VMEM)
smem = pl.BlockSpec(memory_space=pltpu.SMEM)


def limit(mib):
    return pltpu.CompilerParams(vmem_limit_bytes=mib << 20)


def norms_kernel(cent_ref, points_ref, *refs):
    norm_ref = refs[-1]
    for r in range(0, cent_ref.shape[0], tall):
        rows = pl.ds(r, tall)
        entries = cent_ref[rows, :].astype(jnp.float32)
        half_norm = 0.5 * jnp.sum(entries * entries, axis=1, keepdims=True)
        norm_ref[rows, :] = jnp.broadcast_to(half_norm, (tall, lanes))
    logits_kernel(cent_ref, points_ref, norm_ref, *refs[:-1])


def logits_kernel(cent_ref, points_ref, norm_ref, raised_ref, peak_ref, lse_ref):
    n_cent, n_tok = raised_ref.shape
    row_blocks = [pl.ds(r, tall) for r in range(0, n_cent, tall)]
    token_blocks = [pl.ds(t, tile) for t in range(0, n_tok, tile)]
    peaks = []
    for step in range(len(token_blocks) + 1):
        tops, totals = [], []
        for rows in row_blocks:
            if step < len(token_blocks):
                cols = token_blocks[step]
                product = jnp.dot(
                    cent_ref[rows, :], points_ref[:, cols], preferred_element_type=jnp.float32
                )
                logits = sharpness * (product - norm_ref[rows, :1])
                raised_ref[rows, cols] = logits
                tops.append(jnp.max(logits, axis=0, keepdims=True))
            if step > 0:
                cols = token_blocks[step - 1]
                raised = jnp.exp(raised_ref[rows, cols] - peaks[step - 1])
                raised_ref[rows, cols] = raised
                totals.append(jnp.sum(raised, axis=0, keepdims=True))
        if step < len(token_blocks):
            peaks.append(functools.reduce(jnp.maximum, tops))
            peak_ref[:, token_blocks[step]] = peaks[step]
        if step > 0:
            lse_ref[:, token_blocks[step - 1]] = peaks[step - 1] + jnp.log(sum(totals))


def local_softmax(centroids, points, norms=None):
    n_cent, n_tok = centroids.shape[0], points.shape[1]
    row = jax.ShapeDtypeStruct((1, n_tok), jnp.float32)
    outs = (jax.ShapeDtypeStruct((n_cent, n_tok), jnp.float32), row, row)
    if norms is None:
        outs += (jax.ShapeDtypeStruct((n_cent, lanes), jnp.float32),)
    operands = (centroids, points) + (() if norms is None else (norms,))
    results = pl.pallas_call(
        norms_kernel if norms is None else logits_kernel,
        out_shape=outs,
        in_specs=[vmem] * len(operands),
        out_specs=[vmem] * len(outs),
        compiler_params=limit(12),
        cost_estimate=pl.CostEstimate(
            flops=2 * centroids.size * n_tok, bytes_accessed=8 * n_cent * n_tok,
            transcendentals=n_cent * n_tok,
        ),
        name="local_softmax",
    )(*operands)
    return results if norms is None else (*results, norms)


def sums_kernel(order, n_blocks, place_ref, lse_ref, *refs):
    halves, outs, resp_ref = (refs[0:3], refs[3:6]), refs[6:-1], refs[-1]
    depth = halves[0][2].shape[0]
    share = refs[0].shape[0] // n_blocks
    n_tok = refs[0].shape[1]
    far = len(outs) - len(order)
    cut = outs[0].shape[0]

    def put(i, start, value):
        value = value.astype(jnp.bfloat16)
        if i > 0 or not far:
            outs[i + far][pl.ds(start, value.shape[0]), :] = value
        elif start < cut:
            outs[0][pl.ds(start, value.shape[0]), :] = value
        else:
            outs[1][pl.ds(start - cut, value.shape[0]), :] = value

    parts = lse_ref[...]
    top = jnp.max(parts, axis=0, keepdims=True)
    norm = top + jnp.log(jnp.sum(jnp.exp(parts - top), axis=0, keepdims=True))
    scales = [
        jnp.exp(half[1][...] - norm[:, h * n_tok:(h + 1) * n_tok]) for h, half in enumerate(halves)
    ]
    for i, d in enumerate(order):
        start = lax.rem(place_ref[0] + d + n_blocks, n_blocks) * share
        rows = pl.ds(pl.multiple_of(start, share), share)
        count = jnp.zeros((share, 1), jnp.float32)
        for h, half in enumerate(halves):
            resp = (half[0][rows, :] * scales[h]).astype(jnp.bfloat16)
            resp_ref[pl.ds(i * share, share), pl.ds(h * n_tok, n_tok)] = resp
            count += jnp.sum(resp.astype(jnp.float32), axis=1, keepdims=True)
        put(i, depth // lanes * share, jnp.transpose(jnp.broadcast_to(count, (share, lanes)))[:count_rows])
    for i in range(0, len(order), tall // share):
        rows = min(tall, (len(order) - i) * share)
        for c in range(0, depth, tile):
            total = sum(
                lax.dot_general(
                    resp_ref[pl.ds(i * share, rows), pl.ds(h * n_tok, n_tok)],
                    half[2][pl.ds(c, tile), :],
                    (((1,), (1,)), ((), ())),
                    preferred_element_type=jnp.float32,
                )
                for h, half in enumerate(halves)
            )
            for k in range(rows // share):
                for p in range(0, tile, lanes):
                    put(i + k, (c + p) // lanes * share, total[k * share:(k + 1) * share, p:p + lanes])


def weighted_sums(order, n_blocks, far, place, lse, halves):
    n_cent, n_tok = halves[0][0].shape
    depth = halves[0][2].shape[0]
    n = len(order)
    share = n_cent // n_blocks
    height, cut = depth // lanes * share + count_rows, depth // lanes // 2 * share
    heights = ((cut, height - cut) if far else (height,)) + (height,) * (n - 1)
    return pl.pallas_call(
        functools.partial(sums_kernel, order, n_blocks),
        out_shape=tuple(jax.ShapeDtypeStruct((h, lanes), jnp.bfloat16) for h in heights),
        in_specs=[smem] + [vmem] * 7,
        out_specs=(vmem,) * len(heights),
        scratch_shapes=[pltpu.VMEM((n * share, 2 * n_tok), jnp.bfloat16)],
        compiler_params=limit(20),
        cost_estimate=pl.CostEstimate(
            flops=4 * n * share * n_tok * depth, bytes_accessed=16 * n * share * n_tok, transcendentals=0
        ),
        name="weighted_sums",
    )(place, lse, *halves[0], *halves[1])


def finish_kernel(factor, own_ref, down_ref, up_ref, fresh_ref, counts_ref):
    share, depth = fresh_ref.shape

    def total(start, size):
        rows = pl.ds(start, size)
        return sum(ref[rows, :].astype(jnp.float32) for ref in (own_ref, down_ref, up_ref))

    pieces = [total(c // lanes * share, share) for c in range(0, depth, lanes)]
    mean = jnp.sum(sum(piece * piece for piece in pieces), axis=1, keepdims=True) / depth
    scale = lax.rsqrt(mean + epsilon)
    for i, piece in enumerate(pieces):
        fresh_ref[:, pl.ds(i * lanes, lanes)] = (piece * scale).astype(fresh_ref.dtype)
    counts_ref[...] = total(depth // lanes * share, count_rows)[:1] * factor


def finish(own, down, up, share, depth, factor):
    fresh, counts = pl.pallas_call(
        functools.partial(finish_kernel, factor),
        out_shape=(
            jax.ShapeDtypeStruct((share, depth), jnp.bfloat16),
            jax.ShapeDtypeStruct((1, share), jnp.float32),
        ),
        in_specs=[vmem] * 3,
        out_specs=[vmem] * 2,
        compiler_params=limit(4),
        name="finish",
    )(own, down, up)
    return fresh, counts.reshape(share)


def core_swap(value):
    return lax.ppermute(value, "core", [(0, 1), (1, 0)])


def spread(value, axis):
    n = lax.psum(1, axis)
    return lax.all_to_all(jnp.broadcast_to(value[None], (n,) + value.shape), axis, 0, 0)


def gather_half(points):
    n_tok, cols = points.shape
    n_z, n_core = lax.axis_size("z"), lax.axis_size("core")
    part, rows = n_tok // n_core, points.T
    halves = jnp.stack([rows[:, c * part:(c + 1) * part] for c in range(n_core)])
    blocks = jnp.broadcast_to(halves[None], (n_z,) + halves.shape).reshape((n_z * n_core,) + halves.shape[1:])
    slab = lax.all_to_all(blocks, ("z", "core"), 0, 0).reshape(-1, n_tok // n_core)
    return spread(slab, "x").reshape(-1, n_tok // n_core)


def dp_shift(value, d):
    n = lax.axis_size("dp")
    return lax.ppermute(value, "dp", [((i + d) % n, i) for i in range(n)])


def ring_order(n):
    near = [s * d for d in range(n // 2 - 1, 0, -1) for s in (-1, 1)]
    return [n // 2] + near + [0]


def add(block, total, start):
    stop = start + total.shape[0]
    part = block[start:stop].astype(jnp.float32) + total.astype(jnp.float32)
    pieces = [block[:start], part.astype(block.dtype), block[stop:]]
    return jnp.concatenate([p for p in pieces if p.shape[0]], axis=0)


def ring_sum(far, make_near):
    down, up = dp_shift(far[0], 1), dp_shift(far[1], -1)
    starts = 0, far[0].shape[0]
    near = make_near(far[0])
    while len(near) > 1:
        rest = make_near(up) if len(near) == 2 else near[2:]
        down = dp_shift(add(near[0], down, starts[0]), 1)
        up = dp_shift(add(near[1], up, starts[1]), -1)
        near = rest
        starts = 0, 0
    return near[0], down, up


def per_device(points, centroids):
    n_dp = lax.axis_size("dp")
    n_cent = lax.axis_size("x") * lax.axis_size("z") * lax.axis_size("core")
    place = lax.axis_index("dp").astype(jnp.int32).reshape(1)
    points, place = lax.optimization_barrier((points, place))
    mine = gather_half(points)
    other = core_swap(mine)
    raised_0, peak_0, lse_0, norms = local_softmax(centroids, mine)
    raised_1, peak_1, lse_1, _ = local_softmax(centroids, other, norms)
    here = jnp.concatenate([lse_0, lse_1], axis=1)
    there = core_swap(jnp.concatenate([lse_1, lse_0], axis=1))
    lse = spread(jnp.logaddexp(here, there)[0], ("x", "z"))
    halves = ((raised_0, peak_0, mine), (raised_1, peak_1, other))
    order = ring_order(n_dp)
    far = weighted_sums(order[:1], n_dp, True, place, lse, halves)
    rounds = [order[i:i + 2] for i in range(1, n_dp - 3, 2)] + [order[-3:]]

    def make_near(after):
        late, _ = lax.optimization_barrier((lse, after))
        return weighted_sums(rounds.pop(0), n_dp, False, place, late, halves)

    own, down, up = ring_sum(far, make_near)
    factor = centroids.shape[0] * n_cent / (points.shape[0] * n_dp)
    return finish(own, down, up, centroids.shape[0] // n_dp, centroids.shape[1], factor)


def solution(mesh):
    n_dp = mesh.shape["dp"]
    split = (4, mesh.shape["cent"] // 8, 2)
    fine = jax.sharding.Mesh(mesh.devices.reshape((n_dp,) + split), ("dp", "x", "z", "core"))
    cent = ("x", "z", "core")
    in_specs = (P("dp", cent), P(cent, None))
    out_specs = (P(cent + ("dp",), None), P(cent + ("dp",)))
    return jax.shard_map(
        per_device, mesh=fine, in_specs=in_specs, out_specs=out_specs, check_vma=False
    )
```

```python
import functools

import jax
import jax.numpy as jnp
from jax import lax
from jax.experimental import pallas as pl
from jax.experimental.pallas import tpu as pltpu
from jax.sharding import PartitionSpec as P

sharpness = 10.0
epsilon = 1e-12
lanes = 128
tile = 256
tall = 512
short = 256
count_rows = 16
vmem = pl.BlockSpec(memory_space=pltpu.VMEM)
smem = pl.BlockSpec(memory_space=pltpu.SMEM)


def limit(mib):
    return pltpu.CompilerParams(vmem_limit_bytes=mib << 20)


def norms_kernel(cent_ref, points_ref, *refs):
    norm_ref = refs[-1]
    for r in range(0, cent_ref.shape[0], tall):
        rows = pl.ds(r, tall)
        entries = cent_ref[rows, :].astype(jnp.float32)
        half_norm = 0.5 * jnp.sum(entries * entries, axis=1, keepdims=True)
        norm_ref[rows, :] = jnp.broadcast_to(half_norm, (tall, lanes))
    logits_kernel(cent_ref, points_ref, norm_ref, *refs[:-1])


def logits_kernel(cent_ref, points_ref, norm_ref, raised_ref, peak_ref, lse_ref):
    n_cent, n_tok = raised_ref.shape
    row_blocks = [pl.ds(r, short) for r in range(0, n_cent, short)]
    token_blocks = [pl.ds(t, tile) for t in range(0, n_tok, tile)]
    peaks = []
    for step in range(len(token_blocks) + 1):
        tops, totals = [], []
        for rows in row_blocks:
            if step < len(token_blocks):
                cols = token_blocks[step]
                product = jnp.dot(
                    cent_ref[rows, :], points_ref[:, cols], preferred_element_type=jnp.float32
                )
                logits = sharpness * (product - norm_ref[rows, :1])
                raised_ref[rows, cols] = logits
                tops.append(jnp.max(logits, axis=0, keepdims=True))
            if step > 0:
                cols = token_blocks[step - 1]
                raised = jnp.exp(raised_ref[rows, cols] - peaks[step - 1])
                raised_ref[rows, cols] = raised
                totals.append(jnp.sum(raised, axis=0, keepdims=True))
        if step < len(token_blocks):
            peaks.append(functools.reduce(jnp.maximum, tops))
            peak_ref[:, token_blocks[step]] = peaks[step]
        if step > 0:
            lse_ref[:, token_blocks[step - 1]] = peaks[step - 1] + jnp.log(sum(totals))


def local_softmax(centroids, points, norms=None):
    n_cent, n_tok = centroids.shape[0], points.shape[1]
    row = jax.ShapeDtypeStruct((1, n_tok), jnp.float32)
    outs = (jax.ShapeDtypeStruct((n_cent, n_tok), jnp.float32), row, row)
    if norms is None:
        outs += (jax.ShapeDtypeStruct((n_cent, lanes), jnp.float32),)
    operands = (centroids, points) + (() if norms is None else (norms,))
    results = pl.pallas_call(
        norms_kernel if norms is None else logits_kernel,
        out_shape=outs,
        in_specs=[vmem] * len(operands),
        out_specs=[vmem] * len(outs),
        compiler_params=limit(12),
        cost_estimate=pl.CostEstimate(
            flops=2 * centroids.size * n_tok, bytes_accessed=8 * n_cent * n_tok,
            transcendentals=n_cent * n_tok,
        ),
        name="local_softmax",
    )(*operands)
    return results if norms is None else (*results, norms)


def sums_kernel(order, n_blocks, place_ref, lse_ref, *refs):
    halves, outs, resp_ref = (refs[0:3], refs[3:6]), refs[6:-1], refs[-1]
    depth = halves[0][2].shape[0]
    share = refs[0].shape[0] // n_blocks
    n_tok = refs[0].shape[1]
    far = len(outs) - len(order)
    cut = outs[0].shape[0]

    def put(i, start, value):
        value = value.astype(jnp.bfloat16)
        if i > 0 or not far:
            outs[i + far][pl.ds(start, value.shape[0]), :] = value
        elif start < cut:
            outs[0][pl.ds(start, value.shape[0]), :] = value
        else:
            outs[1][pl.ds(start - cut, value.shape[0]), :] = value

    parts = lse_ref[...]
    top = jnp.max(parts, axis=0, keepdims=True)
    norm = top + jnp.log(jnp.sum(jnp.exp(parts - top), axis=0, keepdims=True))
    scales = [
        jnp.exp(half[1][...] - norm[:, h * n_tok:(h + 1) * n_tok]) for h, half in enumerate(halves)
    ]
    for i, d in enumerate(order):
        start = lax.rem(place_ref[0] + d + n_blocks, n_blocks) * share
        rows = pl.ds(pl.multiple_of(start, share), share)
        count = jnp.zeros((share, 1), jnp.float32)
        for h, half in enumerate(halves):
            resp = (half[0][rows, :] * scales[h]).astype(jnp.bfloat16)
            resp_ref[pl.ds(i * share, share), pl.ds(h * n_tok, n_tok)] = resp
            count += jnp.sum(resp.astype(jnp.float32), axis=1, keepdims=True)
        put(i, depth // lanes * share, jnp.transpose(jnp.broadcast_to(count, (share, lanes)))[:count_rows])
    for i in range(0, len(order), tall // share):
        rows = min(tall, (len(order) - i) * share)
        for c in range(0, depth, tile):
            total = sum(
                lax.dot_general(
                    resp_ref[pl.ds(i * share, rows), pl.ds(h * n_tok, n_tok)],
                    half[2][pl.ds(c, tile), :],
                    (((1,), (1,)), ((), ())),
                    preferred_element_type=jnp.float32,
                )
                for h, half in enumerate(halves)
            )
            for k in range(rows // share):
                for p in range(0, tile, lanes):
                    put(i + k, (c + p) // lanes * share, total[k * share:(k + 1) * share, p:p + lanes])


def weighted_sums(order, n_blocks, far, place, lse, halves):
    n_cent, n_tok = halves[0][0].shape
    depth = halves[0][2].shape[0]
    n = len(order)
    share = n_cent // n_blocks
    height, cut = depth // lanes * share + count_rows, depth // lanes // 2 * share
    heights = ((cut, height - cut) if far else (height,)) + (height,) * (n - 1)
    return pl.pallas_call(
        functools.partial(sums_kernel, order, n_blocks),
        out_shape=tuple(jax.ShapeDtypeStruct((h, lanes), jnp.bfloat16) for h in heights),
        in_specs=[smem] + [vmem] * 7,
        out_specs=(vmem,) * len(heights),
        scratch_shapes=[pltpu.VMEM((n * share, 2 * n_tok), jnp.bfloat16)],
        compiler_params=limit(20),
        cost_estimate=pl.CostEstimate(
            flops=4 * n * share * n_tok * depth, bytes_accessed=16 * n * share * n_tok, transcendentals=0
        ),
        name="weighted_sums",
    )(place, lse, *halves[0], *halves[1])


def finish_kernel(factor, own_ref, down_ref, up_ref, fresh_ref, counts_ref):
    share, depth = fresh_ref.shape

    def total(start, size):
        rows = pl.ds(start, size)
        return sum(ref[rows, :].astype(jnp.float32) for ref in (own_ref, down_ref, up_ref))

    pieces = [total(c // lanes * share, share) for c in range(0, depth, lanes)]
    mean = jnp.sum(sum(piece * piece for piece in pieces), axis=1, keepdims=True) / depth
    scale = lax.rsqrt(mean + epsilon)
    for i, piece in enumerate(pieces):
        fresh_ref[:, pl.ds(i * lanes, lanes)] = (piece * scale).astype(fresh_ref.dtype)
    counts_ref[...] = total(depth // lanes * share, count_rows)[:1] * factor


def finish(own, down, up, share, depth, factor):
    fresh, counts = pl.pallas_call(
        functools.partial(finish_kernel, factor),
        out_shape=(
            jax.ShapeDtypeStruct((share, depth), jnp.bfloat16),
            jax.ShapeDtypeStruct((1, share), jnp.float32),
        ),
        in_specs=[vmem] * 3,
        out_specs=[vmem] * 2,
        compiler_params=limit(4),
        name="finish",
    )(own, down, up)
    return fresh, counts.reshape(share)


def core_swap(value):
    return lax.ppermute(value, "core", [(0, 1), (1, 0)])


def spread(value, axis):
    n = lax.psum(1, axis)
    return lax.all_to_all(jnp.broadcast_to(value[None], (n,) + value.shape), axis, 0, 0)


def gather_half(points):
    n_tok, cols = points.shape
    n_z, n_core = lax.axis_size("z"), lax.axis_size("core")
    part, rows = n_tok // n_core, points.T
    halves = jnp.stack([rows[:, c * part:(c + 1) * part] for c in range(n_core)])
    blocks = jnp.broadcast_to(halves[None], (n_z,) + halves.shape).reshape((n_z * n_core,) + halves.shape[1:])
    slab = lax.all_to_all(blocks, ("z", "core"), 0, 0).reshape(-1, n_tok // n_core)
    return spread(slab, "x").reshape(-1, n_tok // n_core)


def dp_shift(value, d):
    n = lax.axis_size("dp")
    return lax.ppermute(value, "dp", [((i + d) % n, i) for i in range(n)])


def ring_order(n):
    near = [s * d for d in range(n // 2 - 1, 0, -1) for s in (-1, 1)]
    return [n // 2] + near + [0]


def add(block, total, start):
    stop = start + total.shape[0]
    part = block[start:stop].astype(jnp.float32) + total.astype(jnp.float32)
    pieces = [block[:start], part.astype(block.dtype), block[stop:]]
    return jnp.concatenate([p for p in pieces if p.shape[0]], axis=0)


def ring_sum(far, make_near):
    down, up = dp_shift(far[0], 1), dp_shift(far[1], -1)
    starts = 0, far[0].shape[0]
    near = make_near(far[0])
    while len(near) > 1:
        rest = make_near(up) if len(near) == 2 else near[2:]
        down = dp_shift(add(near[0], down, starts[0]), 1)
        up = dp_shift(add(near[1], up, starts[1]), -1)
        near = rest
        starts = 0, 0
    return near[0], down, up


def per_device(points, centroids):
    n_dp = lax.axis_size("dp")
    n_cent = lax.axis_size("x") * lax.axis_size("z") * lax.axis_size("core")
    place = lax.axis_index("dp").astype(jnp.int32).reshape(1)
    points, place = lax.optimization_barrier((points, place))
    mine = gather_half(points)
    other = core_swap(mine)
    raised_0, peak_0, lse_0, norms = local_softmax(centroids, mine)
    raised_1, peak_1, lse_1, _ = local_softmax(centroids, other, norms)
    here = jnp.concatenate([lse_0, lse_1], axis=1)
    there = core_swap(jnp.concatenate([lse_1, lse_0], axis=1))
    lse = spread(jnp.logaddexp(here, there)[0], ("x", "z"))
    halves = ((raised_0, peak_0, mine), (raised_1, peak_1, other))
    order = ring_order(n_dp)
    far = weighted_sums(order[:1], n_dp, True, place, lse, halves)
    rounds = [order[i:i + 2] for i in range(1, n_dp - 3, 2)] + [order[-3:]]

    def make_near(after):
        late, _ = lax.optimization_barrier((lse, after))
        return weighted_sums(rounds.pop(0), n_dp, False, place, late, halves)

    own, down, up = ring_sum(far, make_near)
    factor = centroids.shape[0] * n_cent / (points.shape[0] * n_dp)
    return finish(own, down, up, centroids.shape[0] // n_dp, centroids.shape[1], factor)


def solution(mesh):
    n_dp = mesh.shape["dp"]
    split = (4, mesh.shape["cent"] // 8, 2)
    fine = jax.sharding.Mesh(mesh.devices.reshape((n_dp,) + split), ("dp", "x", "z", "core"))
    cent = ("x", "z", "core")
    in_specs = (P("dp", cent), P(cent, None))
    out_specs = (P(cent + ("dp",), None), P(cent + ("dp",)))
    return jax.shard_map(
        per_device, mesh=fine, in_specs=in_specs, out_specs=out_specs, check_vma=False
    )
```

```python
import functools

import jax
import jax.numpy as jnp
from jax import lax
from jax.experimental import pallas as pl
from jax.experimental.pallas import tpu as pltpu
from jax.sharding import PartitionSpec as P

sharpness = 10.0
epsilon = 1e-12
lanes = 128
tile = 256
tall = 512
count_rows = 16
vmem = pl.BlockSpec(memory_space=pltpu.VMEM)
smem = pl.BlockSpec(memory_space=pltpu.SMEM)


def limit(mib):
    return pltpu.CompilerParams(vmem_limit_bytes=mib << 20)


def norms_kernel(cent_ref, points_ref, *refs):
    norm_ref = refs[-1]
    for r in range(0, cent_ref.shape[0], tall):
        rows = pl.ds(r, tall)
        entries = cent_ref[rows, :].astype(jnp.float32)
        half_norm = 0.5 * jnp.sum(entries * entries, axis=1, keepdims=True)
        norm_ref[rows, :] = jnp.broadcast_to(half_norm, (tall, lanes))
    logits_kernel(cent_ref, points_ref, norm_ref, *refs[:-1])


def logits_kernel(cent_ref, points_ref, norm_ref, raised_ref, peak_ref, lse_ref):
    n_cent, n_tok = raised_ref.shape
    row_blocks = [pl.ds(r, tall) for r in range(0, n_cent, tall)]
    token_blocks = [pl.ds(t, tile) for t in range(0, n_tok, tile)]
    peaks = []
    for step in range(len(token_blocks) + 1):
        tops, totals = [], []
        for rows in row_blocks:
            if step < len(token_blocks):
                cols = token_blocks[step]
                product = jnp.dot(
                    cent_ref[rows, :], points_ref[:, cols], preferred_element_type=jnp.float32
                )
                logits = sharpness * (product - norm_ref[rows, :1])
                raised_ref[rows, cols] = logits
                tops.append(jnp.max(logits, axis=0, keepdims=True))
            if step > 0:
                cols = token_blocks[step - 1]
                raised = jnp.exp(raised_ref[rows, cols] - peaks[step - 1])
                raised_ref[rows, cols] = raised
                totals.append(jnp.sum(raised, axis=0, keepdims=True))
        if step < len(token_blocks):
            peaks.append(functools.reduce(jnp.maximum, tops))
            peak_ref[:, token_blocks[step]] = peaks[step]
        if step > 0:
            lse_ref[:, token_blocks[step - 1]] = peaks[step - 1] + jnp.log(sum(totals))


def local_softmax(centroids, points, norms=None):
    n_cent, n_tok = centroids.shape[0], points.shape[1]
    row = jax.ShapeDtypeStruct((1, n_tok), jnp.float32)
    outs = (jax.ShapeDtypeStruct((n_cent, n_tok), jnp.float32), row, row)
    if norms is None:
        outs += (jax.ShapeDtypeStruct((n_cent, lanes), jnp.float32),)
    operands = (centroids, points) + (() if norms is None else (norms,))
    results = pl.pallas_call(
        norms_kernel if norms is None else logits_kernel,
        out_shape=outs,
        in_specs=[vmem] * len(operands),
        out_specs=[vmem] * len(outs),
        compiler_params=limit(12),
        cost_estimate=pl.CostEstimate(
            flops=2 * centroids.size * n_tok, bytes_accessed=8 * n_cent * n_tok,
            transcendentals=n_cent * n_tok,
        ),
        name="local_softmax",
    )(*operands)
    return results if norms is None else (*results, norms)


def sums_kernel(order, n_blocks, span, place_ref, lse_ref, *refs):
    halves, outs, resp_ref = (refs[0:3], refs[3:6]), refs[6:-1], refs[-1]
    depth = halves[0][2].shape[0]
    share = refs[0].shape[0] // n_blocks
    n_tok = refs[0].shape[1]
    top_row = span[0] // lanes * share

    def put(i, start, value):
        outs[i][pl.ds(start - top_row, value.shape[0]), :] = value.astype(jnp.bfloat16)

    parts = lse_ref[...]
    top = jnp.max(parts, axis=0, keepdims=True)
    norm = top + jnp.log(jnp.sum(jnp.exp(parts - top), axis=0, keepdims=True))
    scales = [
        jnp.exp(half[1][...] - norm[:, h * n_tok:(h + 1) * n_tok]) for h, half in enumerate(halves)
    ]
    for i, d in enumerate(order):
        start = lax.rem(place_ref[0] + d + n_blocks, n_blocks) * share
        rows = pl.ds(pl.multiple_of(start, share), share)
        count = jnp.zeros((share, 1), jnp.float32)
        for h, half in enumerate(halves):
            resp = (half[0][rows, :] * scales[h]).astype(jnp.bfloat16)
            resp_ref[pl.ds(i * share, share), pl.ds(h * n_tok, n_tok)] = resp
            count += jnp.sum(resp.astype(jnp.float32), axis=1, keepdims=True)
        if span[1] == depth:
            put(i, depth // lanes * share, jnp.transpose(jnp.broadcast_to(count, (share, lanes)))[:count_rows])
    for i in range(0, len(order), tall // share):
        rows = min(tall, (len(order) - i) * share)
        for c in range(*span, tile):
            total = sum(
                lax.dot_general(
                    resp_ref[pl.ds(i * share, rows), pl.ds(h * n_tok, n_tok)],
                    half[2][pl.ds(c, tile), :],
                    (((1,), (1,)), ((), ())),
                    preferred_element_type=jnp.float32,
                )
                for h, half in enumerate(halves)
            )
            for k in range(rows // share):
                for p in range(0, tile, lanes):
                    put(i + k, (c + p) // lanes * share, total[k * share:(k + 1) * share, p:p + lanes])


def weighted_sums(order, n_blocks, place, lse, halves, span=None):
    n_cent, n_tok = halves[0][0].shape
    depth = halves[0][2].shape[0]
    n = len(order)
    share = n_cent // n_blocks
    span = span or (0, depth)
    height = (span[1] - span[0]) // lanes * share + (count_rows if span[1] == depth else 0)
    return pl.pallas_call(
        functools.partial(sums_kernel, order, n_blocks, span),
        out_shape=(jax.ShapeDtypeStruct((height, lanes), jnp.bfloat16),) * n,
        in_specs=[smem] + [vmem] * 7,
        out_specs=(vmem,) * n,
        scratch_shapes=[pltpu.VMEM((n * share, 2 * n_tok), jnp.bfloat16)],
        compiler_params=limit(20),
        cost_estimate=pl.CostEstimate(
            flops=4 * n * share * n_tok * depth, bytes_accessed=16 * n * share * n_tok, transcendentals=0
        ),
        name="weighted_sums",
    )(place, lse, *halves[0], *halves[1])


def finish_kernel(factor, own_ref, down_ref, up_ref, fresh_ref, counts_ref):
    share, depth = fresh_ref.shape

    def total(start, size):
        rows = pl.ds(start, size)
        return sum(ref[rows, :].astype(jnp.float32) for ref in (own_ref, down_ref, up_ref))

    pieces = [total(c // lanes * share, share) for c in range(0, depth, lanes)]
    mean = jnp.sum(sum(piece * piece for piece in pieces), axis=1, keepdims=True) / depth
    scale = lax.rsqrt(mean + epsilon)
    for i, piece in enumerate(pieces):
        fresh_ref[:, pl.ds(i * lanes, lanes)] = (piece * scale).astype(fresh_ref.dtype)
    counts_ref[...] = total(depth // lanes * share, count_rows)[:1] * factor


def finish(own, down, up, share, depth, factor):
    fresh, counts = pl.pallas_call(
        functools.partial(finish_kernel, factor),
        out_shape=(
            jax.ShapeDtypeStruct((share, depth), jnp.bfloat16),
            jax.ShapeDtypeStruct((1, share), jnp.float32),
        ),
        in_specs=[vmem] * 3,
        out_specs=[vmem] * 2,
        compiler_params=limit(4),
        name="finish",
    )(own, down, up)
    return fresh, counts.reshape(share)


def core_swap(value):
    return lax.ppermute(value, "core", [(0, 1), (1, 0)])


def spread(value, axis):
    n = lax.psum(1, axis)
    return lax.all_to_all(jnp.broadcast_to(value[None], (n,) + value.shape), axis, 0, 0)


def gather_half(points):
    n_tok, cols = points.shape
    n_z, n_core = lax.axis_size("z"), lax.axis_size("core")
    part, rows = n_tok // n_core, points.T
    halves = jnp.stack([rows[:, c * part:(c + 1) * part] for c in range(n_core)])
    blocks = jnp.broadcast_to(halves[None], (n_z,) + halves.shape).reshape((n_z * n_core,) + halves.shape[1:])
    slab = lax.all_to_all(blocks, ("z", "core"), 0, 0).reshape(-1, n_tok // n_core)
    return spread(slab, "x").reshape(-1, n_tok // n_core)


def dp_shift(value, d):
    n = lax.axis_size("dp")
    return lax.ppermute(value, "dp", [((i + d) % n, i) for i in range(n)])


def ring_order(n):
    near = [s * d for d in range(n // 2 - 1, 0, -1) for s in (-1, 1)]
    return [n // 2] + near + [0]


def add(block, total, start):
    stop = start + total.shape[0]
    part = block[start:stop].astype(jnp.float32) + total.astype(jnp.float32)
    pieces = [block[:start], part.astype(block.dtype), block[stop:]]
    return jnp.concatenate([p for p in pieces if p.shape[0]], axis=0)


def ring_sum(far, make_near):
    down, up = dp_shift(far[0], 1), dp_shift(far[1], -1)
    starts = 0, far[0].shape[0]
    near = make_near(far[1])
    while len(near) > 1:
        rest = make_near(up) if len(near) == 2 else near[2:]
        down = dp_shift(add(near[0], down, starts[0]), 1)
        up = dp_shift(add(near[1], up, starts[1]), -1)
        near = rest
        starts = 0, 0
    return near[0], down, up


def per_device(points, centroids):
    n_dp = lax.axis_size("dp")
    n_cent = lax.axis_size("x") * lax.axis_size("z") * lax.axis_size("core")
    place = lax.axis_index("dp").astype(jnp.int32).reshape(1)
    points, place = lax.optimization_barrier((points, place))
    mine = gather_half(points)
    other = core_swap(mine)
    raised_0, peak_0, lse_0, norms = local_softmax(centroids, mine)
    raised_1, peak_1, lse_1, _ = local_softmax(centroids, other, norms)
    here = jnp.concatenate([lse_0, lse_1], axis=1)
    there = core_swap(jnp.concatenate([lse_1, lse_0], axis=1))
    lse = spread(jnp.logaddexp(here, there)[0], ("x", "z"))
    halves = ((raised_0, peak_0, mine), (raised_1, peak_1, other))
    order = ring_order(n_dp)
    depth = centroids.shape[1]
    far = [
        weighted_sums(order[:1], n_dp, place, lse, halves, span)[0]
        for span in ((0, depth // 2), (depth // 2, depth))
    ]
    rounds = [order[i:i + 2] for i in range(1, n_dp - 3, 2)] + [order[-3:]]

    def make_near(after):
        late, _ = lax.optimization_barrier((lse, after))
        return weighted_sums(rounds.pop(0), n_dp, place, late, halves)

    own, down, up = ring_sum(far, make_near)
    factor = centroids.shape[0] * n_cent / (points.shape[0] * n_dp)
    return finish(own, down, up, centroids.shape[0] // n_dp, centroids.shape[1], factor)


def solution(mesh):
    n_dp = mesh.shape["dp"]
    split = (4, mesh.shape["cent"] // 8, 2)
    fine = jax.sharding.Mesh(mesh.devices.reshape((n_dp,) + split), ("dp", "x", "z", "core"))
    cent = ("x", "z", "core")
    in_specs = (P("dp", cent), P(cent, None))
    out_specs = (P(cent + ("dp",), None), P(cent + ("dp",)))
    return jax.shard_map(
        per_device, mesh=fine, in_specs=in_specs, out_specs=out_specs, check_vma=False
    )
```

```python
import functools

import jax
import jax.numpy as jnp
from jax import lax
from jax.experimental import pallas as pl
from jax.experimental.pallas import tpu as pltpu
from jax.sharding import PartitionSpec as P

sharpness = 10.0
epsilon = 1e-12
lanes = 128
tile = 256
tall = 512
count_rows = 16
vmem = pl.BlockSpec(memory_space=pltpu.VMEM)
smem = pl.BlockSpec(memory_space=pltpu.SMEM)


def limit(mib):
    return pltpu.CompilerParams(vmem_limit_bytes=mib << 20)


def norms_kernel(cent_ref, points_ref, *refs):
    norm_ref = refs[-1]
    for r in range(0, cent_ref.shape[0], tall):
        rows = pl.ds(r, tall)
        entries = cent_ref[rows, :].astype(jnp.float32)
        half_norm = 0.5 * jnp.sum(entries * entries, axis=1, keepdims=True)
        norm_ref[rows, :] = jnp.broadcast_to(half_norm, (tall, lanes))
    logits_kernel(cent_ref, points_ref, norm_ref, *refs[:-1])


def logits_kernel(cent_ref, points_ref, norm_ref, raised_ref, peak_ref, lse_ref):
    n_cent, n_tok = raised_ref.shape
    row_blocks = [pl.ds(r, tall) for r in range(0, n_cent, tall)]
    token_blocks = [pl.ds(t, tile) for t in range(0, n_tok, tile)]
    peaks = []
    for step in range(len(token_blocks) + 1):
        tops, totals = [], []
        for rows in row_blocks:
            if step < len(token_blocks):
                cols = token_blocks[step]
                product = jnp.dot(
                    cent_ref[rows, :], points_ref[:, cols], preferred_element_type=jnp.float32
                )
                logits = sharpness * (product - norm_ref[rows, :1])
                raised_ref[rows, cols] = logits
                tops.append(jnp.max(logits, axis=0, keepdims=True))
            if step > 0:
                cols = token_blocks[step - 1]
                raised = jnp.exp(raised_ref[rows, cols] - peaks[step - 1])
                raised_ref[rows, cols] = raised
                totals.append(jnp.sum(raised, axis=0, keepdims=True))
        if step < len(token_blocks):
            peaks.append(functools.reduce(jnp.maximum, tops))
            peak_ref[:, token_blocks[step]] = peaks[step]
        if step > 0:
            lse_ref[:, token_blocks[step - 1]] = peaks[step - 1] + jnp.log(sum(totals))


def local_softmax(centroids, points, norms=None):
    n_cent, n_tok = centroids.shape[0], points.shape[1]
    row = jax.ShapeDtypeStruct((1, n_tok), jnp.float32)
    outs = (jax.ShapeDtypeStruct((n_cent, n_tok), jnp.float32), row, row)
    if norms is None:
        outs += (jax.ShapeDtypeStruct((n_cent, lanes), jnp.float32),)
    operands = (centroids, points) + (() if norms is None else (norms,))
    results = pl.pallas_call(
        norms_kernel if norms is None else logits_kernel,
        out_shape=outs,
        in_specs=[vmem] * len(operands),
        out_specs=[vmem] * len(outs),
        compiler_params=limit(12),
        cost_estimate=pl.CostEstimate(
            flops=2 * centroids.size * n_tok, bytes_accessed=8 * n_cent * n_tok,
            transcendentals=n_cent * n_tok,
        ),
        name="local_softmax",
    )(*operands)
    return results if norms is None else (*results, norms)


def sums_kernel(order, n_blocks, place_ref, lse_ref, *refs):
    halves, outs, resp_ref = (refs[0:3], refs[3:6]), refs[6:-1], refs[-1]
    depth = halves[0][2].shape[0]
    share = refs[0].shape[0] // n_blocks
    n_tok = refs[0].shape[1]
    far = len(outs) - len(order)
    cut = outs[0].shape[0]

    def put(i, start, value):
        value = value.astype(jnp.bfloat16)
        if i > 0 or not far:
            outs[i + far][pl.ds(start, value.shape[0]), :] = value
        elif start < cut:
            outs[0][pl.ds(start, value.shape[0]), :] = value
        else:
            outs[1][pl.ds(start - cut, value.shape[0]), :] = value

    parts = lse_ref[...]
    top = jnp.max(parts, axis=0, keepdims=True)
    norm = top + jnp.log(jnp.sum(jnp.exp(parts - top), axis=0, keepdims=True))
    scales = [
        jnp.exp(half[1][...] - norm[:, h * n_tok:(h + 1) * n_tok]) for h, half in enumerate(halves)
    ]
    for i, d in enumerate(order):
        start = lax.rem(place_ref[0] + d + n_blocks, n_blocks) * share
        rows = pl.ds(pl.multiple_of(start, share), share)
        count = jnp.zeros((share, 1), jnp.float32)
        for h, half in enumerate(halves):
            resp = (half[0][rows, :] * scales[h]).astype(jnp.bfloat16)
            resp_ref[pl.ds(i * share, share), pl.ds(h * n_tok, n_tok)] = resp
            count += jnp.sum(resp.astype(jnp.float32), axis=1, keepdims=True)
        put(i, depth // lanes * share, jnp.transpose(jnp.broadcast_to(count, (share, lanes)))[:count_rows])
    for i in range(0, len(order), tall // share):
        rows = min(tall, (len(order) - i) * share)
        for c in range(0, depth, tile):
            total = sum(
                lax.dot_general(
                    resp_ref[pl.ds(i * share, rows), pl.ds(h * n_tok, n_tok)],
                    half[2][pl.ds(c, tile), :],
                    (((1,), (1,)), ((), ())),
                    preferred_element_type=jnp.float32,
                )
                for h, half in enumerate(halves)
            )
            for k in range(rows // share):
                for p in range(0, tile, lanes):
                    put(i + k, (c + p) // lanes * share, total[k * share:(k + 1) * share, p:p + lanes])


def weighted_sums(order, n_blocks, far, place, lse, halves):
    n_cent, n_tok = halves[0][0].shape
    depth = halves[0][2].shape[0]
    n = len(order)
    share = n_cent // n_blocks
    height, cut = depth // lanes * share + count_rows, depth // lanes // 2 * share
    heights = ((cut, height - cut) if far else (height,)) + (height,) * (n - 1)
    return pl.pallas_call(
        functools.partial(sums_kernel, order, n_blocks),
        out_shape=tuple(jax.ShapeDtypeStruct((h, lanes), jnp.bfloat16) for h in heights),
        in_specs=[smem] + [vmem] * 7,
        out_specs=(vmem,) * len(heights),
        scratch_shapes=[pltpu.VMEM((n * share, 2 * n_tok), jnp.bfloat16)],
        compiler_params=limit(20),
        cost_estimate=pl.CostEstimate(
            flops=4 * n * share * n_tok * depth, bytes_accessed=16 * n * share * n_tok, transcendentals=0
        ),
        name="weighted_sums",
    )(place, lse, *halves[0], *halves[1])


def finish_kernel(factor, own_ref, down_ref, up_ref, fresh_ref, counts_ref):
    share, depth = fresh_ref.shape

    def total(start, size):
        rows = pl.ds(start, size)
        return sum(ref[rows, :].astype(jnp.float32) for ref in (own_ref, down_ref, up_ref))

    pieces = [total(c // lanes * share, share) for c in range(0, depth, lanes)]
    mean = jnp.sum(sum(piece * piece for piece in pieces), axis=1, keepdims=True) / depth
    scale = lax.rsqrt(mean + epsilon)
    for i, piece in enumerate(pieces):
        fresh_ref[:, pl.ds(i * lanes, lanes)] = (piece * scale).astype(fresh_ref.dtype)
    counts_ref[...] = total(depth // lanes * share, count_rows)[:1] * factor


def finish(own, down, up, share, depth, factor):
    fresh, counts = pl.pallas_call(
        functools.partial(finish_kernel, factor),
        out_shape=(
            jax.ShapeDtypeStruct((share, depth), jnp.bfloat16),
            jax.ShapeDtypeStruct((1, share), jnp.float32),
        ),
        in_specs=[vmem] * 3,
        out_specs=[vmem] * 2,
        compiler_params=limit(4),
        name="finish",
    )(own, down, up)
    return fresh, counts.reshape(share)


def core_swap(value):
    return lax.ppermute(value, "core", [(0, 1), (1, 0)])


def spread(value, axis):
    n = lax.psum(1, axis)
    return lax.all_to_all(jnp.broadcast_to(value[None], (n,) + value.shape), axis, 0, 0)


def gather_half(points):
    n_tok, cols = points.shape
    n_z, n_core = lax.axis_size("z"), lax.axis_size("core")
    part, rows = n_tok // n_core, points.T
    halves = jnp.stack([rows[:, c * part:(c + 1) * part] for c in range(n_core)])
    blocks = jnp.broadcast_to(halves[None], (n_z,) + halves.shape).reshape((n_z * n_core,) + halves.shape[1:])
    slab = lax.all_to_all(blocks, ("z", "core"), 0, 0).reshape(-1, n_tok // n_core)
    return spread(slab, "x").reshape(-1, n_tok // n_core)


def dp_shift(value, d):
    n = lax.axis_size("dp")
    return lax.ppermute(value, "dp", [((i + d) % n, i) for i in range(n)])


def ring_order(n):
    near = [s * d for d in range(n // 2 - 1, 0, -1) for s in (-1, 1)]
    return [n // 2] + near + [0]


def add(block, total, start):
    stop = start + total.shape[0]
    part = block[start:stop].astype(jnp.float32) + total.astype(jnp.float32)
    pieces = [block[:start], part.astype(block.dtype), block[stop:]]
    return jnp.concatenate([p for p in pieces if p.shape[0]], axis=0)


def ring_sum(far, make_near):
    down, up = dp_shift(far[0], 1), dp_shift(far[1], -1)
    starts = 0, far[0].shape[0]
    near = make_near(far[0])
    while len(near) > 1:
        rest = make_near(up)
        down = dp_shift(add(near[0], down, starts[0]), 1)
        up = dp_shift(add(near[1], up, starts[1]), -1)
        near = rest
        starts = 0, 0
    return near[0], down, up


def per_device(points, centroids):
    n_dp = lax.axis_size("dp")
    n_cent = lax.axis_size("x") * lax.axis_size("z") * lax.axis_size("core")
    place = lax.axis_index("dp").astype(jnp.int32).reshape(1)
    points, place = lax.optimization_barrier((points, place))
    mine = gather_half(points)
    other = core_swap(mine)
    raised_0, peak_0, lse_0, norms = local_softmax(centroids, mine)
    raised_1, peak_1, lse_1, _ = local_softmax(centroids, other, norms)
    here = jnp.concatenate([lse_0, lse_1], axis=1)
    there = core_swap(jnp.concatenate([lse_1, lse_0], axis=1))
    lse = spread(jnp.logaddexp(here, there)[0], ("x", "z"))
    halves = ((raised_0, peak_0, mine), (raised_1, peak_1, other))
    order = ring_order(n_dp)
    far = weighted_sums(order[:1], n_dp, True, place, lse, halves)
    rounds = [order[i:i + 2] for i in range(1, n_dp - 1, 2)] + [order[-1:]]

    def make_near(after):
        late, _ = lax.optimization_barrier((lse, after))
        return weighted_sums(rounds.pop(0), n_dp, False, place, late, halves)

    own, down, up = ring_sum(far, make_near)
    factor = centroids.shape[0] * n_cent / (points.shape[0] * n_dp)
    return finish(own, down, up, centroids.shape[0] // n_dp, centroids.shape[1], factor)


def solution(mesh):
    n_dp = mesh.shape["dp"]
    split = (4, mesh.shape["cent"] // 8, 2)
    fine = jax.sharding.Mesh(mesh.devices.reshape((n_dp,) + split), ("dp", "x", "z", "core"))
    cent = ("x", "z", "core")
    in_specs = (P("dp", cent), P(cent, None))
    out_specs = (P(cent + ("dp",), None), P(cent + ("dp",)))
    return jax.shard_map(
        per_device, mesh=fine, in_specs=in_specs, out_specs=out_specs, check_vma=False
    )
```
